32 devices in a mesh: leaf: 16 (over z, y, x), front: 2 (over core).
Axes of the slice: x: 2, y: 2, z: 4, core: 2. Of those that a mesh axis runs over, the one named last changes fastest.
Arguments:
- child_pivot: float32 [32, 1152, 1152], P('leaf', 'front'), as said below
- child_lower: float32 [32, 192, 1152], P('leaf', 'front'), as said below
- child_tail: float32 [32, 192, 192], P('leaf', 'front'), as said below
- child_map: int32 [32, 192], replicated, may hold values from 0 to 1151, as said below
- child_parent: int32 [32, 1], replicated, may hold values from 0 to 15, as said below
- owner: int32 [16], replicated, may hold values from 0 to 15, as said below
- parent_front: float32 [16, 1152, 1152], P('leaf', 'front'), as said below
Outputs:
- child_diag: float32 [32, 1152, 1152], P('leaf', 'front')
- child_below: float32 [32, 192, 1152], P('leaf', 'front')
- parent_factor: float32 [16, 1152, 1152], P('leaf', 'front')
The draws below stay inside these ranges and needn't reach their ends.
Inputs may be any that keep to these rules, and one draw needn't show every extreme that they name: For each child c the symmetric matrix with blocks child_pivot[c], child_lower[c]^T in the upper right, child_lower[c] and child_tail[c] is positive definite, with camera blocks of 6 rows and columns. `child_lower`: same matrices as stated for child_pivot. `child_tail`: same matrices as stated for child_pivot. Each parent_front[g] is symmetric positive definite. `child_map`: within one child the entries are distinct; entries k * 192 // 2 to (k + 1) * 192 // 2 - 1 lie in k * 1152 // 2 to (k + 1) * 1152 // 2 - 1, for k below 2. `child_parent`: every parent has at least one child. Child 2 * g, the first child of leaf group g, has a parent owned by group (g + 8) mod 16; the other children's parents are spread unevenly. `owner`: each leaf group owns exactly one parent.
All inputs are finite; a program needn't handle non-finite values.
Results may differ from the reference program's by a relative error of at most 0.00005.
Values sent between devices are 32-bit elements; how exact they have to be, the bound alone decides.
A program may use at most 192 MiB of HBM per device.

```python
import jax
import jax.numpy as jnp
from jax import lax

P_SIZE = 1152
FP = 1152
C = 192
CHILDREN = 32
PARENTS = 16
N_FRONT = 2


def front_matrix(seed_key, order):
    part_keys = jax.random.split(seed_key, 3)
    normal_part = jax.random.normal(part_keys[0], (order, order), jnp.float32)
    normal_part = (normal_part + normal_part.T) * 0.7071
    cameras = order // 6
    picks = jax.random.randint(part_keys[1], (cameras, cameras), 0, 128)
    picks = jnp.minimum(picks, picks.T)
    strong = jnp.where(picks < 2, 1.0, 0.0).astype(jnp.float32)
    strong = jnp.repeat(jnp.repeat(strong, 6, axis=0), 6, axis=1)
    offdiag = normal_part * (0.02 + strong) * (1.0 - jnp.eye(order, dtype=jnp.float32))
    rowsum = jnp.sum(jnp.abs(offdiag), axis=1)
    margin = jax.random.uniform(part_keys[2], (order,), jnp.float32, 0.05, 1.0)
    matrix = (offdiag + jnp.diag(1.02 * rowsum + margin * (1.0 + 0.02 * rowsum))) * (25.0 / order)
    return matrix


def child_fronts(seed_key):
    child_keys = jax.random.split(jax.random.fold_in(seed_key, 11), CHILDREN)
    return lax.map(lambda one_key: front_matrix(one_key, P_SIZE + C), child_keys)


def draw_child_pivot(key, part):
    return child_fronts(key)[:, :P_SIZE, :P_SIZE]


def draw_child_lower(key, part):
    return child_fronts(key)[:, P_SIZE:, :P_SIZE]


def draw_child_tail(key, part):
    return child_fronts(key)[:, P_SIZE:, P_SIZE:]


def draw_parent_front(key, part):
    parent_keys = jax.random.split(jax.random.fold_in(key, 23), PARENTS)
    return lax.map(lambda one_key: front_matrix(one_key, FP), parent_keys)


def draw_child_map(key, part):
    rows_per_block = FP // N_FRONT
    used_per_block = C // N_FRONT
    map_keys = jax.random.split(jax.random.fold_in(key, 37), CHILDREN * N_FRONT)
    picks = jax.vmap(lambda one_key: jax.random.permutation(one_key, rows_per_block)[:used_per_block])(map_keys)
    offsets = (jnp.arange(N_FRONT, dtype=jnp.int32) * rows_per_block)[None, :, None]
    picks = picks.astype(jnp.int32).reshape(CHILDREN, N_FRONT, used_per_block) + offsets
    return picks.reshape(CHILDREN, C).astype(jnp.int32)


def owner_table(key):
    return jax.random.permutation(jax.random.fold_in(key, 51), PARENTS).astype(jnp.int32)


def draw_owner(key, part):
    return owner_table(key)


def draw_child_parent(key, part):
    owners = owner_table(key)
    groups = jnp.arange(PARENTS, dtype=jnp.int32)
    inverse = jnp.zeros((PARENTS,), jnp.int32).at[owners].set(groups)
    far_group = (groups + PARENTS // 2) % PARENTS
    first_kid = inverse[far_group]
    kid_count = CHILDREN // PARENTS
    first_pick = jax.random.randint(jax.random.fold_in(key, 53), (PARENTS, kid_count), 0, PARENTS)
    second_pick = jax.random.randint(jax.random.fold_in(key, 59), (PARENTS, kid_count), 0, PARENTS)
    others = jnp.minimum(first_pick, second_pick).astype(jnp.int32)
    is_first = (jnp.arange(kid_count, dtype=jnp.int32) == 0)[None, :]
    parents = jnp.where(is_first, first_kid[:, None], others)
    return parents.reshape(CHILDREN, 1).astype(jnp.int32)


def setup_inputs(seed: int = 0) -> dict:
    key_of = jax.random.split(jax.random.key(seed), 8)
    return {
        "child_pivot": draw_child_pivot(jax.random.fold_in(key_of[7], 71), 0),
        "child_lower": draw_child_lower(jax.random.fold_in(key_of[7], 71), 0),
        "child_tail": draw_child_tail(jax.random.fold_in(key_of[7], 71), 0),
        "child_map": draw_child_map(jax.random.fold_in(key_of[7], 71), 0),
        "child_parent": draw_child_parent(jax.random.fold_in(key_of[7], 71), 0),
        "owner": draw_owner(jax.random.fold_in(key_of[7], 71), 0),
        "parent_front": draw_parent_front(jax.random.fold_in(key_of[7], 71), 0),
    }


def eliminate_child(blocks):
    pivot_block, lower_block, tail_block = blocks
    diag_rows = jnp.linalg.cholesky(pivot_block)
    below_rows = jax.scipy.linalg.solve_triangular(diag_rows, lower_block.T, lower=True).T
    schur = tail_block - jnp.dot(below_rows.astype(jnp.float32), below_rows.T.astype(jnp.float32), precision=lax.Precision.HIGHEST, preferred_element_type=jnp.float32)
    return (diag_rows, below_rows, schur)

def reference(child_pivot, child_lower, child_tail, child_map, child_parent, owner, parent_front):
    diag_rows, below_rows, schur = lax.map(eliminate_child, (child_pivot, child_lower, child_tail))
    owner_slot = owner[child_parent[:, 0]].astype(jnp.int32)
    row_index = child_map[:, :, None]
    col_index = child_map[:, None, :]
    assembled = parent_front.at[owner_slot[:, None, None], row_index, col_index].add(schur)
    parent_factor = lax.map(jnp.linalg.cholesky, assembled)
    return (diag_rows, below_rows, parent_factor)
```

```python
import functools

import jax
import jax.numpy as jnp
from jax import lax
from jax.experimental import pallas as pl
from jax.experimental.pallas import tpu as pltpu
from jax.sharding import PartitionSpec as P

NB = 128
PW = 16
F32 = jnp.float32
BF16 = jnp.bfloat16


def split(x):
    high = x.astype(BF16)
    low = (x - high.astype(F32)).astype(BF16)
    return high, low


def rows_dot(a, b):
    return lax.dot_general(a, b, (((1,), (1,)), ((), ())), preferred_element_type=F32)


def cols_dot(a, b):
    return lax.dot_general(a, b, (((0,), (0,)), ((), ())), preferred_element_type=F32)


def factor_block(work):
    row = lax.broadcasted_iota(jnp.int32, (PW, NB), 0)
    for panel in range(NB // PW):
        first = panel * PW
        left = work[first : first + PW, :NB]
        right = work[first : first + PW, NB:]
        cols = [
            jnp.broadcast_to(left[:, first + j : first + j + 1], (PW, NB)) for j in range(PW)
        ]
        for j in range(PW):
            inv = lax.rsqrt(jnp.broadcast_to(cols[j][j : j + 1], (PW, NB)))
            scaled = jnp.where(row > j, cols[j] * inv, 0.0)
            left_row = jnp.broadcast_to(left[j : j + 1], (PW, NB)) * inv
            right_row = jnp.broadcast_to(right[j : j + 1], (PW, NB)) * inv
            left = jnp.where(row == j, left_row, left - scaled * left_row)
            right = jnp.where(row == j, right_row, right - scaled * right_row)
            for k in range(j + 1, PW):
                cols[k] = cols[k] - scaled * (
                    jnp.broadcast_to(cols[k][j : j + 1], (PW, NB)) * inv
                )
        work[first : first + PW, :NB] = left
        work[first : first + PW, NB:] = right
        if first + PW < NB:
            left_high, left_low = split(left)
            right_high, right_low = split(right)
            both_high = jnp.concatenate([left_high, right_high], axis=1)
            both_low = jnp.concatenate([left_low, right_low], axis=1)
            update = cols_dot(
                jnp.concatenate([left_high, left_high, left_low], axis=0),
                jnp.concatenate([both_high, both_low, both_high], axis=0),
            )
            work[first + PW :, :] = work[first + PW :, :] - update[first + PW :, :]


def factor_front(front, panel, work, pivots, rows):
    blocks = pivots // NB
    row = lax.broadcasted_iota(jnp.int32, (NB, NB), 0)
    col = lax.broadcasted_iota(jnp.int32, (NB, NB), 1)

    def step(block, carry):
        base = pl.multiple_of(block * NB, NB)
        work[:, :NB] = front[pl.ds(base, NB), pl.ds(base, NB)]
        work[:, NB:] = jnp.where(row == col, 1.0, 0.0)
        factor_block(work)
        front[pl.ds(base, NB), pl.ds(base, NB)] = jnp.where(
            row >= col, jnp.transpose(work[:, :NB]), 0.0
        )
        inv_high, inv_low = split(work[:, NB:])
        inv_twice = jnp.concatenate([inv_high, inv_high], axis=1)
        for at in range(blocks):

            @pl.when(block == at)
            def _():
                here = at * NB
                after = here + NB
                if at:
                    front[:here, here:after] = jnp.zeros((here, NB), F32)
                if after >= rows:
                    return
                high, low = split(front[after:rows, here:after])
                solved = rows_dot(jnp.concatenate([high, low], axis=1), inv_twice)
                solved = solved + rows_dot(high, inv_low)
                front[after:rows, here:after] = solved
                high, low = split(solved)
                panel[after:rows, :NB] = high
                panel[after:rows, NB:] = low

                def tile(index, carry):
                    start = pl.multiple_of(after + index * 2 * NB, NB)
                    col_high = panel[pl.ds(start, 2 * NB), :NB]
                    col_low = panel[pl.ds(start, 2 * NB), NB:]
                    update = rows_dot(
                        panel[after:rows, :], jnp.concatenate([col_high, col_high], axis=1)
                    )
                    update = update + rows_dot(panel[after:rows, :NB], col_low)
                    front[after:rows, pl.ds(start, 2 * NB)] = (
                        front[after:rows, pl.ds(start, 2 * NB)] - update
                    )
                    return carry

                lax.fori_loop(0, -(-(rows - after) // (2 * NB)), tile, 0)

        return carry

    lax.fori_loop(0, blocks, step, 0)


def padded(rows):
    return -(-rows // NB) * NB + NB


def child_kernel(
    own_p, got_p, own_l, got_l, own_t, got_t, diag, diag_send, below, below_send, schur,
    front, panel, work, tail, sems,
):
    member = lax.axis_index("front")
    half = own_p.shape[1]
    pivots = half * 2
    half_c = own_l.shape[1]
    contrib = half_c * 2
    rows = pivots + contrib
    mine = pl.multiple_of(member * half, 8)
    theirs = pl.multiple_of((1 - member) * half, 8)
    mine_c = pl.multiple_of(member * half_c, 8)
    theirs_c = pl.multiple_of((1 - member) * half_c, 8)
    pivot_cols = pl.ds(0, pivots)
    copies = [
        pltpu.make_async_copy(own_p.at[member], front.at[pl.ds(mine, half), pivot_cols], sems.at[0]),
        pltpu.make_async_copy(got_p, front.at[pl.ds(theirs, half), pivot_cols], sems.at[1]),
        pltpu.make_async_copy(
            own_l.at[member], front.at[pl.ds(pivots + mine_c, half_c), pivot_cols], sems.at[2]
        ),
        pltpu.make_async_copy(
            got_l, front.at[pl.ds(pivots + theirs_c, half_c), pivot_cols], sems.at[3]
        ),
        pltpu.make_async_copy(own_t.at[member], tail.at[pl.ds(mine_c, half_c)], sems.at[4]),
        pltpu.make_async_copy(got_t, tail.at[pl.ds(theirs_c, half_c)], sems.at[5]),
    ]
    for copy in copies:
        copy.start()
    for copy in copies:
        copy.wait()
    front[pivots:rows, pivots:rows] = tail[...]
    factor_front(front, panel, work, pivots, rows)
    schur[...] = front[pivots:rows, pivots:rows]
    copies = [
        pltpu.make_async_copy(front.at[pl.ds(mine, half), pivot_cols], diag.at[member], sems.at[0]),
        pltpu.make_async_copy(front.at[pl.ds(theirs, half), pivot_cols], diag_send, sems.at[1]),
        pltpu.make_async_copy(
            front.at[pl.ds(pivots + mine_c, half_c), pivot_cols], below.at[member], sems.at[2]
        ),
        pltpu.make_async_copy(
            front.at[pl.ds(pivots + theirs_c, half_c), pivot_cols], below_send, sems.at[3]
        ),
    ]
    for copy in copies:
        copy.start()
    for copy in copies:
        copy.wait()


def eliminate_child(own_p, got_p, own_l, got_l, own_t, got_t):
    half, pivots = got_p.shape
    half_c, contrib = got_t.shape
    rows = pivots + contrib
    anywhere = pl.BlockSpec(memory_space=pl.ANY)
    return pl.pallas_call(
        child_kernel,
        out_shape=(
            jax.ShapeDtypeStruct(own_p.shape, F32),
            jax.ShapeDtypeStruct(got_p.shape, F32),
            jax.ShapeDtypeStruct(own_l.shape, F32),
            jax.ShapeDtypeStruct(got_l.shape, F32),
            jax.ShapeDtypeStruct((contrib, contrib), F32),
        ),
        in_specs=[anywhere] * 6,
        out_specs=(anywhere,) * 4 + (pl.BlockSpec(memory_space=pltpu.VMEM),),
        scratch_shapes=[
            pltpu.VMEM((rows, padded(rows)), F32),
            pltpu.VMEM((padded(rows), 2 * NB), BF16),
            pltpu.VMEM((NB, 2 * NB), F32),
            pltpu.VMEM((contrib, contrib), F32),
            pltpu.SemaphoreType.DMA((6,)),
        ],
        compiler_params=pltpu.CompilerParams(vmem_limit_bytes=48 * 2**20),
    )(own_p, got_p, own_l, got_l, own_t, got_t)


def parent_kernel(
    count, picked, first, maps, own, got, first_schur, others, out,
    front, panel, work, block, sems,
):
    member = lax.axis_index("front")
    half, pivots = got.shape
    contrib = first_schur.shape[0]
    mine = pl.multiple_of(member * half, 8)
    theirs = pl.multiple_of((1 - member) * half, 8)
    pivot_cols = pl.ds(0, pivots)
    copies = [
        pltpu.make_async_copy(own.at[0], front.at[pl.ds(mine, half), pivot_cols], sems.at[0]),
        pltpu.make_async_copy(got, front.at[pl.ds(theirs, half), pivot_cols], sems.at[1]),
    ]
    for copy in copies:
        copy.start()
    for copy in copies:
        copy.wait()
    slot = lax.broadcasted_iota(jnp.int32, (pivots, contrib), 0)
    strip = 3 * NB

    def place(child, values):
        places = jnp.where(slot == maps[pl.ds(child, 1), :], 1.0, 0.0).astype(BF16)
        high, low = split(values)
        spread_high = rows_dot(high, places).astype(BF16)
        spread_low = rows_dot(low, places).astype(BF16)
        for row in range(0, pivots, strip):
            for col in range(0, row + strip, strip):
                chosen = places[row : row + strip]
                front[row : row + strip, col : col + strip] = (
                    front[row : row + strip, col : col + strip]
                    + jnp.dot(
                        chosen, spread_high[:, col : col + strip], preferred_element_type=F32
                    )
                    + jnp.dot(chosen, spread_low[:, col : col + strip], preferred_element_type=F32)
                )

    block[...] = first_schur[...]

    def add(position, carry):
        @pl.when(position > 0)
        def _():
            source = picked[jnp.maximum(position - 1, 0)]
            copy = pltpu.make_async_copy(others.at[source], block, sems.at[0])
            copy.start()
            copy.wait()

        child = jnp.where(
            position > 0, picked[jnp.maximum(position - 1, 0)] * 2 + 1, first[0] * 2
        )
        place(child, block[...])
        return carry

    lax.fori_loop(0, count[0] + 1, add, 0)
    factor_front(front, panel, work, pivots, pivots)
    copy = pltpu.make_async_copy(front.at[pl.ds(mine, half), pivot_cols], out.at[0], sems.at[0])
    copy.start()
    copy.wait()


def eliminate_parent(count, picked, first, maps, own, got, first_schur, others):
    half, pivots = got.shape
    contrib = first_schur.shape[0]
    anywhere = pl.BlockSpec(memory_space=pl.ANY)
    scalars = pl.BlockSpec(memory_space=pltpu.SMEM)
    vmem = pl.BlockSpec(memory_space=pltpu.VMEM)
    return pl.pallas_call(
        parent_kernel,
        out_shape=jax.ShapeDtypeStruct(own.shape, F32),
        in_specs=[scalars] * 3 + [vmem, anywhere, anywhere, vmem, anywhere],
        out_specs=anywhere,
        scratch_shapes=[
            pltpu.VMEM((pivots, padded(pivots)), F32),
            pltpu.VMEM((padded(pivots), 2 * NB), BF16),
            pltpu.VMEM((NB, 2 * NB), F32),
            pltpu.VMEM((contrib, contrib), F32),
            pltpu.SemaphoreType.DMA((2,)),
        ],
        compiler_params=pltpu.CompilerParams(vmem_limit_bytes=48 * 2**20),
    )(count, picked, first, maps, own, got, first_schur, others)


def on_device(child_pivot, child_lower, child_tail, child_map, child_parent, owner, parent_front):
    member = lax.axis_index("front")
    group = lax.axis_index("leaf")
    groups = lax.axis_size("leaf")
    swap = [(0, 1), (1, 0)]

    def theirs(array):
        return lax.dynamic_index_in_dim(array, 1 - member, 0, keepdims=False)

    got_pivot = lax.ppermute(theirs(child_pivot), "front", swap)
    got_lower = lax.ppermute(theirs(child_lower), "front", swap)
    got_tail = lax.ppermute(theirs(child_tail), "front", swap)
    got_parent = lax.ppermute(parent_front[0], "front", swap)
    diag, diag_send, below, below_send, schur = eliminate_child(
        child_pivot, got_pivot, child_lower, got_lower, child_tail, got_tail
    )
    other_schur = lax.ppermute(schur, "front", swap)
    schur_first = jnp.where(member == 0, schur, other_schur)
    schur_second = jnp.where(member == 0, other_schur, schur)
    half_c = schur.shape[0] // 2
    contrib = schur.shape[1]
    far = [(g, (g + groups // 2) % groups) for g in range(groups)]
    first_schur = lax.ppermute(schur_first, "leaf", far)
    part = lax.dynamic_slice_in_dim(schur_second, member * half_c, half_c, 0)
    others = lax.all_gather(part, ("leaf", "front"), axis=0, tiled=True)
    others = others.reshape(groups, contrib, contrib)
    diag_got = lax.ppermute(diag_send, "front", swap)
    below_got = lax.ppermute(below_send, "front", swap)

    mine = owner[child_parent[1::2, 0]] == group
    positions = jnp.arange(groups, dtype=jnp.int32)
    earlier = positions[None, :] < positions[:, None]
    rank = jnp.sum((earlier & mine[None, :]).astype(jnp.int32), axis=1)
    picked = jnp.sum(
        jnp.where((rank[None, :] == positions[:, None]) & mine[None, :], positions[None, :], 0),
        axis=1,
    ).astype(jnp.int32)
    count = jnp.sum(mine.astype(jnp.int32)).reshape(1)
    first = ((group + groups - groups // 2) % groups).astype(jnp.int32).reshape(1)
    parent = eliminate_parent(
        count, picked, first, child_map, parent_front, got_parent, first_schur, others
    )
    diag = lax.dynamic_update_index_in_dim(diag, diag_got, 1 - member, 0)
    below = lax.dynamic_update_index_in_dim(below, below_got, 1 - member, 0)
    return (diag, below, parent)


def solution(mesh):
    in_specs = (
        P("leaf", "front", None),
        P("leaf", "front", None),
        P("leaf", "front", None),
        P(),
        P(),
        P(),
        P("leaf", "front", None),
    )
    out_specs = (P("leaf", "front", None), P("leaf", "front", None), P("leaf", "front", None))
    return jax.shard_map(
        on_device, mesh=mesh, in_specs=in_specs, out_specs=out_specs, check_vma=False
    )
```

```python
import functools
import itertools

import jax
import jax.numpy as jnp
from jax import lax
from jax.experimental import pallas as pl
from jax.experimental.pallas import tpu as pltpu
from jax.sharding import PartitionSpec as P

NB = 128
PW = 16
F32 = jnp.float32
BF16 = jnp.bfloat16


def split(x):
    high = x.astype(BF16)
    low = (x - high.astype(F32)).astype(BF16)
    return high, low


def rows_dot(a, b):
    return lax.dot_general(a, b, (((1,), (1,)), ((), ())), preferred_element_type=F32)


def cols_dot(a, b):
    return lax.dot_general(a, b, (((0,), (0,)), ((), ())), preferred_element_type=F32)


def factor_block(work):
    row = lax.broadcasted_iota(jnp.int32, (PW, NB), 0)
    for panel in range(NB // PW):
        first = panel * PW
        left = work[first : first + PW, :NB]
        right = work[first : first + PW, NB:]
        cols = [
            jnp.broadcast_to(left[:, first + j : first + j + 1], (PW, NB)) for j in range(PW)
        ]
        for j in range(PW):
            inv = lax.rsqrt(jnp.broadcast_to(cols[j][j : j + 1], (PW, NB)))
            scaled = jnp.where(row > j, cols[j] * inv, 0.0)
            left_row = jnp.broadcast_to(left[j : j + 1], (PW, NB)) * inv
            right_row = jnp.broadcast_to(right[j : j + 1], (PW, NB)) * inv
            left = jnp.where(row == j, left_row, left - scaled * left_row)
            right = jnp.where(row == j, right_row, right - scaled * right_row)
            for k in range(j + 1, PW):
                cols[k] = cols[k] - scaled * (
                    jnp.broadcast_to(cols[k][j : j + 1], (PW, NB)) * inv
                )
        work[first : first + PW, :NB] = left
        work[first : first + PW, NB:] = right
        if first + PW < NB:
            left_high, left_low = split(left)
            right_high, right_low = split(right)
            both_high = jnp.concatenate([left_high, right_high], axis=1)
            both_low = jnp.concatenate([left_low, right_low], axis=1)
            update = cols_dot(
                jnp.concatenate([left_high, left_high, left_low], axis=0),
                jnp.concatenate([both_high, both_low, both_high], axis=0),
            )
            work[first + PW :, :] = work[first + PW :, :] - update[first + PW :, :]


def factor_front(front, panel, work, pivots, rows):
    blocks = pivots // NB
    row = lax.broadcasted_iota(jnp.int32, (NB, NB), 0)
    col = lax.broadcasted_iota(jnp.int32, (NB, NB), 1)

    def step(block, carry):
        base = pl.multiple_of(block * NB, NB)
        work[:, :NB] = front[pl.ds(base, NB), pl.ds(base, NB)]
        work[:, NB:] = jnp.where(row == col, 1.0, 0.0)
        factor_block(work)
        front[pl.ds(base, NB), pl.ds(base, NB)] = jnp.where(
            row >= col, jnp.transpose(work[:, :NB]), 0.0
        )
        inv_high, inv_low = split(work[:, NB:])
        inv_twice = jnp.concatenate([inv_high, inv_high], axis=1)
        for at in range(blocks):

            @pl.when(block == at)
            def _():
                here = at * NB
                after = here + NB
                if at:
                    front[:here, here:after] = jnp.zeros((here, NB), F32)
                if after >= rows:
                    return
                high, low = split(front[after:rows, here:after])
                solved = rows_dot(jnp.concatenate([high, low], axis=1), inv_twice)
                solved = solved + rows_dot(high, inv_low)
                front[after:rows, here:after] = solved
                high, low = split(solved)
                panel[after:rows, :NB] = high
                panel[after:rows, NB:] = low

                def tile(index, carry):
                    start = pl.multiple_of(after + index * 2 * NB, NB)
                    col_high = panel[pl.ds(start, 2 * NB), :NB]
                    col_low = panel[pl.ds(start, 2 * NB), NB:]
                    update = rows_dot(
                        panel[after:rows, :], jnp.concatenate([col_high, col_high], axis=1)
                    )
                    update = update + rows_dot(panel[after:rows, :NB], col_low)
                    front[after:rows, pl.ds(start, 2 * NB)] = (
                        front[after:rows, pl.ds(start, 2 * NB)] - update
                    )
                    return carry

                lax.fori_loop(0, -(-(rows - after) // (2 * NB)), tile, 0)

        return carry

    lax.fori_loop(0, blocks, step, 0)


def padded(rows):
    return -(-rows // NB) * NB + NB


def pack(front, packed, start, contrib):
    third = contrib // 3
    a, b, c, end = start, start + third, start + 2 * third, start + contrib
    packed[:third, :] = jnp.concatenate([front[a:b, a:b], front[b:c, b:c]], axis=1)
    packed[third : 2 * third, :] = front[c:end, a:c]
    packed[2 * third :, :] = jnp.concatenate([front[b:c, a:b], front[c:end, c:end]], axis=1)


def unpack(packed):
    third = packed.shape[0] // 3
    diag, last, mixed = packed[:third], packed[third : 2 * third], packed[2 * third :]
    last_t = jnp.transpose(last)
    mixed_t = jnp.transpose(mixed)
    top = jnp.concatenate([diag[:, :third], mixed_t[:third], last_t[:third]], axis=1)
    middle = jnp.concatenate([mixed[:, :third], diag[:, third:], last_t[third:]], axis=1)
    bottom = jnp.concatenate([last, mixed_t[third:]], axis=1)
    return jnp.concatenate([top, middle, bottom], axis=0)


def exchange_kernel(
    groups, packed, first, others, swap, held, swap_sems, first_sems, send_sems, recv_sems,
    front_send, front_recv,
):
    member = lax.axis_index("front")
    group = lax.axis_index("leaf")
    half = packed.shape[0] // 2
    mine = pl.multiple_of(member * half, 8)
    theirs = pl.multiple_of((1 - member) * half, 8)
    rows = pl.ds(mine, half)
    strides = []
    stride = groups
    while stride > 1:
        stride = stride // 4
        strides.append(stride)
    digits = [(group // stride) % 4 for stride in strides]

    def at(shifts):
        return sum(
            ((digit + shift) % 4) * stride
            for digit, shift, stride in zip(digits, shifts, strides)
        )

    def unit(stage, shift):
        return tuple(shift if s == stage else 0 for s in range(len(strides)))

    other_core = {"front": 1 - member}
    mesh = pl.DeviceIdType.MESH
    barrier = pltpu.get_barrier_semaphore()
    pl.semaphore_signal(barrier, inc=1, device_id=other_core, device_id_type=mesh)
    for stage in range(len(strides)):
        for shift in range(1, 4):
            pl.semaphore_signal(
                barrier, inc=1, device_id={"leaf": at(unit(stage, shift))}, device_id_type=mesh
            )
    pl.semaphore_wait(barrier, 1 + 3 * len(strides))

    def remote(src, dst, send_sem, recv_sem, device):
        return pltpu.make_async_remote_copy(
            src_ref=src,
            dst_ref=dst,
            send_sem=send_sem,
            recv_sem=recv_sem,
            device_id=device,
            device_id_type=mesh,
        )

    started = []
    swapped = remote(
        packed.at[pl.ds(theirs, half)], swap, swap_sems.at[0], swap_sems.at[1], other_core
    )
    swapped.start()
    swapped.wait()
    own = packed[rows, :]
    got = swap[...]
    held[...] = jnp.where(member == 0, own, got)
    others[group, rows, :] = jnp.where(member == 0, got, own)

    sent = 0
    arrivals = {}
    order = sorted(
        itertools.product(range(4), repeat=len(strides)),
        key=lambda shifts: max([s for s in range(len(strides)) if shifts[s]], default=-1),
    )
    first_copy = None
    for shifts in order:
        block = at(shifts)
        stage = max([s for s in range(len(strides)) if shifts[s]], default=-1)
        here = others.at[block, rows]
        if stage >= 0:
            remote(here, here, send_sems.at[0], recv_sems.at[block], other_core).wait_recv()
        for later in range(stage + 1, len(strides)):
            for shift in (2, 1, 3):
                copy = remote(
                    here, here, send_sems.at[sent], recv_sems.at[block],
                    {"leaf": at(unit(later, shift))},
                )
                copy.start()
                started.append(copy)
                sent += 1
            if stage < 0 and later == 0:
                first_copy = remote(
                    held, first.at[rows], first_sems.at[0], first_sems.at[1],
                    {"leaf": at(unit(0, 2))},
                )
                first_copy.start()
        across = remote(here, here, front_send.at[block], front_recv.at[block], other_core)
        across.start()
        arrivals[shifts] = across
    first_copy.wait_recv()
    first_across = remote(
        first.at[rows], first.at[rows], first_sems.at[2], first_sems.at[3], other_core
    )
    first_across.start()
    first_copy.wait_send()
    for copy in started:
        copy.wait_send()
    theirs_rows = pl.ds(theirs, half)
    for shifts, across in arrivals.items():
        block = at(shifts)
        across.wait_send()
        there = others.at[block, theirs_rows]
        remote(there, there, front_send.at[block], front_recv.at[block], other_core).wait_recv()
    first_across.wait_send()
    there = first.at[theirs_rows]
    remote(there, there, first_sems.at[2], first_sems.at[3], other_core).wait_recv()


def exchange(packed, groups):
    rows, cols = packed.shape
    vmem = pl.BlockSpec(memory_space=pltpu.VMEM)
    return pl.pallas_call(
        functools.partial(exchange_kernel, groups),
        out_shape=(
            jax.ShapeDtypeStruct((rows, cols), F32),
            jax.ShapeDtypeStruct((groups, rows, cols), F32),
        ),
        in_specs=[vmem],
        out_specs=(vmem, vmem),
        scratch_shapes=[
            pltpu.VMEM((rows // 2, cols), F32),
            pltpu.VMEM((rows // 2, cols), F32),
            pltpu.SemaphoreType.DMA((2,)),
            pltpu.SemaphoreType.DMA((4,)),
            pltpu.SemaphoreType.DMA((groups,)),
            pltpu.SemaphoreType.DMA((groups,)),
            pltpu.SemaphoreType.DMA((groups,)),
            pltpu.SemaphoreType.DMA((groups,)),
        ],
        compiler_params=pltpu.CompilerParams(
            collective_id=0, has_side_effects=True, vmem_limit_bytes=40 * 2**20
        ),
    )(packed)


def child_kernel(
    own_p, got_p, own_l, got_l, own_t, got_t, diag, diag_send, below, below_send, schur,
    front, panel, work, tail, sems,
):
    member = lax.axis_index("front")
    half = own_p.shape[1]
    pivots = half * 2
    half_c = own_l.shape[1]
    contrib = half_c * 2
    rows = pivots + contrib
    mine = pl.multiple_of(member * half, 8)
    theirs = pl.multiple_of((1 - member) * half, 8)
    mine_c = pl.multiple_of(member * half_c, 8)
    theirs_c = pl.multiple_of((1 - member) * half_c, 8)
    pivot_cols = pl.ds(0, pivots)
    copies = [
        pltpu.make_async_copy(own_p.at[member], front.at[pl.ds(mine, half), pivot_cols], sems.at[0]),
        pltpu.make_async_copy(got_p, front.at[pl.ds(theirs, half), pivot_cols], sems.at[1]),
        pltpu.make_async_copy(
            own_l.at[member], front.at[pl.ds(pivots + mine_c, half_c), pivot_cols], sems.at[2]
        ),
        pltpu.make_async_copy(
            got_l, front.at[pl.ds(pivots + theirs_c, half_c), pivot_cols], sems.at[3]
        ),
        pltpu.make_async_copy(own_t.at[member], tail.at[pl.ds(mine_c, half_c)], sems.at[4]),
        pltpu.make_async_copy(got_t, tail.at[pl.ds(theirs_c, half_c)], sems.at[5]),
    ]
    for copy in copies:
        copy.start()
    for copy in copies:
        copy.wait()
    front[pivots:rows, pivots:rows] = tail[...]
    factor_front(front, panel, work, pivots, rows)
    pack(front, schur, pivots, contrib)
    copies = [
        pltpu.make_async_copy(front.at[pl.ds(mine, half), pivot_cols], diag.at[member], sems.at[0]),
        pltpu.make_async_copy(front.at[pl.ds(theirs, half), pivot_cols], diag_send, sems.at[1]),
        pltpu.make_async_copy(
            front.at[pl.ds(pivots + mine_c, half_c), pivot_cols], below.at[member], sems.at[2]
        ),
        pltpu.make_async_copy(
            front.at[pl.ds(pivots + theirs_c, half_c), pivot_cols], below_send, sems.at[3]
        ),
    ]
    for copy in copies:
        copy.start()
    for copy in copies:
        copy.wait()


def eliminate_child(own_p, got_p, own_l, got_l, own_t, got_t):
    half, pivots = got_p.shape
    half_c, contrib = got_t.shape
    rows = pivots + contrib
    anywhere = pl.BlockSpec(memory_space=pl.ANY)
    return pl.pallas_call(
        child_kernel,
        out_shape=(
            jax.ShapeDtypeStruct(own_p.shape, F32),
            jax.ShapeDtypeStruct(got_p.shape, F32),
            jax.ShapeDtypeStruct(own_l.shape, F32),
            jax.ShapeDtypeStruct(got_l.shape, F32),
            jax.ShapeDtypeStruct((contrib, 2 * (contrib // 3)), F32),
        ),
        in_specs=[anywhere] * 6,
        out_specs=(anywhere,) * 4 + (pl.BlockSpec(memory_space=pltpu.VMEM),),
        scratch_shapes=[
            pltpu.VMEM((rows, padded(rows)), F32),
            pltpu.VMEM((padded(rows), 2 * NB), BF16),
            pltpu.VMEM((NB, 2 * NB), F32),
            pltpu.VMEM((contrib, contrib), F32),
            pltpu.SemaphoreType.DMA((6,)),
        ],
        compiler_params=pltpu.CompilerParams(vmem_limit_bytes=48 * 2**20),
    )(own_p, got_p, own_l, got_l, own_t, got_t)


def parent_kernel(
    count, picked, first, maps, own, got, first_schur, others, out,
    front, panel, work, block, sems,
):
    member = lax.axis_index("front")
    half, pivots = got.shape
    contrib = first_schur.shape[0]
    mine = pl.multiple_of(member * half, 8)
    theirs = pl.multiple_of((1 - member) * half, 8)
    pivot_cols = pl.ds(0, pivots)
    copies = [
        pltpu.make_async_copy(own.at[0], front.at[pl.ds(mine, half), pivot_cols], sems.at[0]),
        pltpu.make_async_copy(got, front.at[pl.ds(theirs, half), pivot_cols], sems.at[1]),
    ]
    for copy in copies:
        copy.start()
    for copy in copies:
        copy.wait()
    slot = lax.broadcasted_iota(jnp.int32, (pivots, contrib), 0)
    strip = 3 * NB

    def place(child, values):
        places = jnp.where(slot == maps[pl.ds(child, 1), :], 1.0, 0.0).astype(BF16)
        high, low = split(values)
        spread_high = rows_dot(high, places).astype(BF16)
        spread_low = rows_dot(low, places).astype(BF16)
        for row in range(0, pivots, strip):
            for col in range(0, row + strip, strip):
                chosen = places[row : row + strip]
                front[row : row + strip, col : col + strip] = (
                    front[row : row + strip, col : col + strip]
                    + jnp.dot(
                        chosen, spread_high[:, col : col + strip], preferred_element_type=F32
                    )
                    + jnp.dot(chosen, spread_low[:, col : col + strip], preferred_element_type=F32)
                )

    block[...] = first_schur[...]

    def add(position, carry):
        @pl.when(position > 0)
        def _():
            source = picked[jnp.maximum(position - 1, 0)]
            copy = pltpu.make_async_copy(others.at[source], block, sems.at[0])
            copy.start()
            copy.wait()

        child = jnp.where(
            position > 0, picked[jnp.maximum(position - 1, 0)] * 2 + 1, first[0] * 2
        )
        place(child, unpack(block[...]))
        return carry

    lax.fori_loop(0, count[0] + 1, add, 0)
    factor_front(front, panel, work, pivots, pivots)
    copy = pltpu.make_async_copy(front.at[pl.ds(mine, half), pivot_cols], out.at[0], sems.at[0])
    copy.start()
    copy.wait()


def eliminate_parent(count, picked, first, maps, own, got, first_schur, others):
    half, pivots = got.shape
    anywhere = pl.BlockSpec(memory_space=pl.ANY)
    scalars = pl.BlockSpec(memory_space=pltpu.SMEM)
    vmem = pl.BlockSpec(memory_space=pltpu.VMEM)
    return pl.pallas_call(
        parent_kernel,
        out_shape=jax.ShapeDtypeStruct(own.shape, F32),
        in_specs=[scalars] * 3 + [vmem, anywhere, anywhere, vmem, anywhere],
        out_specs=anywhere,
        scratch_shapes=[
            pltpu.VMEM((pivots, padded(pivots)), F32),
            pltpu.VMEM((padded(pivots), 2 * NB), BF16),
            pltpu.VMEM((NB, 2 * NB), F32),
            pltpu.VMEM(first_schur.shape, F32),
            pltpu.SemaphoreType.DMA((2,)),
        ],
        compiler_params=pltpu.CompilerParams(vmem_limit_bytes=48 * 2**20),
    )(count, picked, first, maps, own, got, first_schur, others)


def on_device(child_pivot, child_lower, child_tail, child_map, child_parent, owner, parent_front):
    member = lax.axis_index("front")
    group = lax.axis_index("leaf")
    groups = lax.axis_size("leaf")
    swap = [(0, 1), (1, 0)]

    def theirs(array):
        return lax.dynamic_index_in_dim(array, 1 - member, 0, keepdims=False)

    got_pivot = lax.ppermute(theirs(child_pivot), "front", swap)
    got_lower = lax.ppermute(theirs(child_lower), "front", swap)
    got_tail = lax.ppermute(theirs(child_tail), "front", swap)
    got_parent = lax.ppermute(parent_front[0], "front", swap)
    diag, diag_send, below, below_send, schur = eliminate_child(
        child_pivot, got_pivot, child_lower, got_lower, child_tail, got_tail
    )
    first_schur, others = exchange(schur, groups)
    diag_got = lax.ppermute(diag_send, "front", swap)
    below_got = lax.ppermute(below_send, "front", swap)

    mine = owner[child_parent[1::2, 0]] == group
    positions = jnp.arange(groups, dtype=jnp.int32)
    earlier = positions[None, :] < positions[:, None]
    rank = jnp.sum((earlier & mine[None, :]).astype(jnp.int32), axis=1)
    picked = jnp.sum(
        jnp.where((rank[None, :] == positions[:, None]) & mine[None, :], positions[None, :], 0),
        axis=1,
    ).astype(jnp.int32)
    count = jnp.sum(mine.astype(jnp.int32)).reshape(1)
    first = ((group + groups - groups // 2) % groups).astype(jnp.int32).reshape(1)
    parent = eliminate_parent(
        count, picked, first, child_map, parent_front, got_parent, first_schur, others
    )
    diag = lax.dynamic_update_index_in_dim(diag, diag_got, 1 - member, 0)
    below = lax.dynamic_update_index_in_dim(below, below_got, 1 - member, 0)
    return (diag, below, parent)


def solution(mesh):
    in_specs = (
        P("leaf", "front", None),
        P("leaf", "front", None),
        P("leaf", "front", None),
        P(),
        P(),
        P(),
        P("leaf", "front", None),
    )
    out_specs = (P("leaf", "front", None), P("leaf", "front", None), P("leaf", "front", None))
    return jax.shard_map(
        on_device, mesh=mesh, in_specs=in_specs, out_specs=out_specs, check_vma=False
    )
```

```python
import functools
import itertools

import jax
import jax.numpy as jnp
from jax import lax
from jax.experimental import pallas as pl
from jax.experimental.pallas import tpu as pltpu
from jax.sharding import PartitionSpec as P

NB = 128
PW = 16
F32 = jnp.float32
BF16 = jnp.bfloat16


def split(x):
    high = x.astype(BF16)
    low = (x - high.astype(F32)).astype(BF16)
    return high, low


def rows_dot(a, b):
    return lax.dot_general(a, b, (((1,), (1,)), ((), ())), preferred_element_type=F32)


def cols_dot(a, b):
    return lax.dot_general(a, b, (((0,), (0,)), ((), ())), preferred_element_type=F32)


def factor_block(work):
    row = lax.broadcasted_iota(jnp.int32, (PW, NB), 0)
    for panel in range(NB // PW):
        first = panel * PW
        left = work[first : first + PW, :NB]
        right = work[first : first + PW, NB:]
        cols = [
            jnp.broadcast_to(left[:, first + j : first + j + 1], (PW, NB)) for j in range(PW)
        ]
        for j in range(PW):
            inv = lax.rsqrt(jnp.broadcast_to(cols[j][j : j + 1], (PW, NB)))
            scaled = jnp.where(row > j, cols[j] * inv, 0.0)
            left_row = jnp.broadcast_to(left[j : j + 1], (PW, NB)) * inv
            right_row = jnp.broadcast_to(right[j : j + 1], (PW, NB)) * inv
            left = jnp.where(row == j, left_row, left - scaled * left_row)
            right = jnp.where(row == j, right_row, right - scaled * right_row)
            for k in range(j + 1, PW):
                cols[k] = cols[k] - scaled * (
                    jnp.broadcast_to(cols[k][j : j + 1], (PW, NB)) * inv
                )
        work[first : first + PW, :NB] = left
        work[first : first + PW, NB:] = right
        if first + PW < NB:
            left_high, left_low = split(left)
            right_high, right_low = split(right)
            both_high = jnp.concatenate([left_high, right_high], axis=1)
            both_low = jnp.concatenate([left_low, right_low], axis=1)
            update = cols_dot(
                jnp.concatenate([left_high, left_high, left_low], axis=0),
                jnp.concatenate([both_high, both_low, both_high], axis=0),
            )
            work[first + PW :, :] = work[first + PW :, :] - update[first + PW :, :]


def factor_front(front, panel, work, pivots, rows):
    blocks = pivots // NB
    row = lax.broadcasted_iota(jnp.int32, (NB, NB), 0)
    col = lax.broadcasted_iota(jnp.int32, (NB, NB), 1)

    def step(block, carry):
        base = pl.multiple_of(block * NB, NB)
        work[:, :NB] = front[pl.ds(base, NB), pl.ds(base, NB)]
        work[:, NB:] = jnp.where(row == col, 1.0, 0.0)
        factor_block(work)
        front[pl.ds(base, NB), pl.ds(base, NB)] = jnp.where(
            row >= col, jnp.transpose(work[:, :NB]), 0.0
        )
        inv_high, inv_low = split(work[:, NB:])
        inv_twice = jnp.concatenate([inv_high, inv_high], axis=1)
        for at in range(blocks):

            @pl.when(block == at)
            def _():
                here = at * NB
                after = here + NB
                if at:
                    front[:here, here:after] = jnp.zeros((here, NB), F32)
                if after >= rows:
                    return
                high, low = split(front[after:rows, here:after])
                solved = rows_dot(jnp.concatenate([high, low], axis=1), inv_twice)
                solved = solved + rows_dot(high, inv_low)
                front[after:rows, here:after] = solved
                high, low = split(solved)
                panel[after:rows, :NB] = high
                panel[after:rows, NB:] = low

                def tile(index, carry):
                    start = pl.multiple_of(after + index * 2 * NB, NB)
                    col_high = panel[pl.ds(start, 2 * NB), :NB]
                    col_low = panel[pl.ds(start, 2 * NB), NB:]
                    update = rows_dot(
                        panel[after:rows, :], jnp.concatenate([col_high, col_high], axis=1)
                    )
                    update = update + rows_dot(panel[after:rows, :NB], col_low)
                    front[after:rows, pl.ds(start, 2 * NB)] = (
                        front[after:rows, pl.ds(start, 2 * NB)] - update
                    )
                    return carry

                lax.fori_loop(0, -(-(rows - after) // (2 * NB)), tile, 0)

        return carry

    lax.fori_loop(0, blocks, step, 0)


def padded(rows):
    return -(-rows // NB) * NB + NB


def pack(front, packed, start, contrib):
    third = contrib // 3
    a, b, c, end = start, start + third, start + 2 * third, start + contrib
    packed[:third, :] = jnp.concatenate([front[a:b, a:b], front[b:c, b:c]], axis=1)
    packed[third : 2 * third, :] = front[c:end, a:c]
    packed[2 * third :, :] = jnp.concatenate([front[b:c, a:b], front[c:end, c:end]], axis=1)


def unpack(packed):
    third = packed.shape[0] // 3
    diag, last, mixed = packed[:third], packed[third : 2 * third], packed[2 * third :]
    last_t = jnp.transpose(last)
    mixed_t = jnp.transpose(mixed)
    top = jnp.concatenate([diag[:, :third], mixed_t[:third], last_t[:third]], axis=1)
    middle = jnp.concatenate([mixed[:, :third], diag[:, third:], last_t[third:]], axis=1)
    bottom = jnp.concatenate([last, mixed_t[third:]], axis=1)
    return jnp.concatenate([top, middle, bottom], axis=0)


def exchange_kernel(
    groups, packed, first, others, swap, held, swap_sems, first_sems, send_sems, recv_sems,
    front_send, front_recv,
):
    member = lax.axis_index("front")
    group = lax.axis_index("leaf")
    half = packed.shape[0] // 2
    mine = pl.multiple_of(member * half, 8)
    theirs = pl.multiple_of((1 - member) * half, 8)
    rows = pl.ds(mine, half)
    strides = []
    stride = groups
    while stride > 1:
        stride = stride // 4
        strides.append(stride)
    digits = [(group // stride) % 4 for stride in strides]

    def at(shifts):
        return sum(
            ((digit + shift) % 4) * stride
            for digit, shift, stride in zip(digits, shifts, strides)
        )

    def unit(stage, shift):
        return tuple(shift if s == stage else 0 for s in range(len(strides)))

    other_core = {"front": 1 - member}
    mesh = pl.DeviceIdType.MESH
    barrier = pltpu.get_barrier_semaphore()
    pl.semaphore_signal(barrier, inc=1, device_id=other_core, device_id_type=mesh)
    for stage in range(len(strides)):
        for shift in range(1, 4):
            pl.semaphore_signal(
                barrier, inc=1, device_id={"leaf": at(unit(stage, shift))}, device_id_type=mesh
            )
    pl.semaphore_wait(barrier, 1 + 3 * len(strides))

    def remote(src, dst, send_sem, recv_sem, device):
        return pltpu.make_async_remote_copy(
            src_ref=src,
            dst_ref=dst,
            send_sem=send_sem,
            recv_sem=recv_sem,
            device_id=device,
            device_id_type=mesh,
        )

    started = []
    swapped = remote(
        packed.at[pl.ds(theirs, half)], swap, swap_sems.at[0], swap_sems.at[1], other_core
    )
    swapped.start()
    swapped.wait()
    own = packed[rows, :]
    got = swap[...]
    held[...] = jnp.where(member == 0, own, got)
    others[group, rows, :] = jnp.where(member == 0, got, own)

    sent = 0
    arrivals = {}
    order = sorted(
        itertools.product(range(4), repeat=len(strides)),
        key=lambda shifts: max([s for s in range(len(strides)) if shifts[s]], default=-1),
    )
    first_copy = None
    for shifts in order:
        block = at(shifts)
        stage = max([s for s in range(len(strides)) if shifts[s]], default=-1)
        here = others.at[block, rows]
        if stage >= 0:
            remote(here, here, send_sems.at[0], recv_sems.at[block], other_core).wait_recv()
        for later in range(stage + 1, len(strides)):
            for shift in (2, 1, 3):
                copy = remote(
                    here, here, send_sems.at[sent], recv_sems.at[block],
                    {"leaf": at(unit(later, shift))},
                )
                copy.start()
                started.append(copy)
                sent += 1
            if stage < 0 and later == 0:
                first_copy = remote(
                    held, first.at[rows], first_sems.at[0], first_sems.at[1],
                    {"leaf": at(unit(0, 2))},
                )
                first_copy.start()
        across = remote(here, here, front_send.at[block], front_recv.at[block], other_core)
        across.start()
        arrivals[shifts] = across
    first_copy.wait_recv()
    first_across = remote(
        first.at[rows], first.at[rows], first_sems.at[2], first_sems.at[3], other_core
    )
    first_across.start()
    first_copy.wait_send()
    for copy in started:
        copy.wait_send()
    theirs_rows = pl.ds(theirs, half)
    for shifts, across in arrivals.items():
        block = at(shifts)
        across.wait_send()
        there = others.at[block, theirs_rows]
        remote(there, there, front_send.at[block], front_recv.at[block], other_core).wait_recv()
    first_across.wait_send()
    there = first.at[theirs_rows]
    remote(there, there, first_sems.at[2], first_sems.at[3], other_core).wait_recv()


def exchange(packed, groups):
    rows, cols = packed.shape
    vmem = pl.BlockSpec(memory_space=pltpu.VMEM)
    return pl.pallas_call(
        functools.partial(exchange_kernel, groups),
        out_shape=(
            jax.ShapeDtypeStruct((rows, cols), F32),
            jax.ShapeDtypeStruct((groups, rows, cols), F32),
        ),
        in_specs=[vmem],
        out_specs=(vmem, vmem),
        scratch_shapes=[
            pltpu.VMEM((rows // 2, cols), F32),
            pltpu.VMEM((rows // 2, cols), F32),
            pltpu.SemaphoreType.DMA((2,)),
            pltpu.SemaphoreType.DMA((4,)),
            pltpu.SemaphoreType.DMA((groups,)),
            pltpu.SemaphoreType.DMA((groups,)),
            pltpu.SemaphoreType.DMA((groups,)),
            pltpu.SemaphoreType.DMA((groups,)),
        ],
        compiler_params=pltpu.CompilerParams(
            collective_id=0, has_side_effects=True, vmem_limit_bytes=40 * 2**20
        ),
    )(packed)


def child_kernel(
    own_p, got_p, own_l, got_l, own_t, got_t, diag, diag_send, below, below_send, schur,
    front, panel, work, tail, sems,
):
    member = lax.axis_index("front")
    half = own_p.shape[1]
    pivots = half * 2
    half_c = own_l.shape[1]
    contrib = half_c * 2
    rows = pivots + contrib
    mine = pl.multiple_of(member * half, 8)
    theirs = pl.multiple_of((1 - member) * half, 8)
    mine_c = pl.multiple_of(member * half_c, 8)
    theirs_c = pl.multiple_of((1 - member) * half_c, 8)
    pivot_cols = pl.ds(0, pivots)
    copies = [
        pltpu.make_async_copy(own_p.at[member], front.at[pl.ds(mine, half), pivot_cols], sems.at[0]),
        pltpu.make_async_copy(got_p, front.at[pl.ds(theirs, half), pivot_cols], sems.at[1]),
        pltpu.make_async_copy(
            own_l.at[member], front.at[pl.ds(pivots + mine_c, half_c), pivot_cols], sems.at[2]
        ),
        pltpu.make_async_copy(
            got_l, front.at[pl.ds(pivots + theirs_c, half_c), pivot_cols], sems.at[3]
        ),
        pltpu.make_async_copy(own_t.at[member], tail.at[pl.ds(mine_c, half_c)], sems.at[4]),
        pltpu.make_async_copy(got_t, tail.at[pl.ds(theirs_c, half_c)], sems.at[5]),
    ]
    for copy in copies:
        copy.start()
    for copy in copies:
        copy.wait()
    front[pivots:rows, pivots:rows] = tail[...]
    factor_front(front, panel, work, pivots, rows)
    pack(front, schur, pivots, contrib)
    copies = [
        pltpu.make_async_copy(front.at[pl.ds(mine, half), pivot_cols], diag.at[member], sems.at[0]),
        pltpu.make_async_copy(front.at[pl.ds(theirs, half), pivot_cols], diag_send, sems.at[1]),
        pltpu.make_async_copy(
            front.at[pl.ds(pivots + mine_c, half_c), pivot_cols], below.at[member], sems.at[2]
        ),
        pltpu.make_async_copy(
            front.at[pl.ds(pivots + theirs_c, half_c), pivot_cols], below_send, sems.at[3]
        ),
    ]
    for copy in copies:
        copy.start()
    for copy in copies:
        copy.wait()


def eliminate_child(own_p, got_p, own_l, got_l, own_t, got_t):
    half, pivots = got_p.shape
    half_c, contrib = got_t.shape
    rows = pivots + contrib
    anywhere = pl.BlockSpec(memory_space=pl.ANY)
    return pl.pallas_call(
        child_kernel,
        out_shape=(
            jax.ShapeDtypeStruct(own_p.shape, F32),
            jax.ShapeDtypeStruct(got_p.shape, F32),
            jax.ShapeDtypeStruct(own_l.shape, F32),
            jax.ShapeDtypeStruct(got_l.shape, F32),
            jax.ShapeDtypeStruct((contrib, 2 * (contrib // 3)), F32),
        ),
        in_specs=[anywhere] * 6,
        out_specs=(anywhere,) * 4 + (pl.BlockSpec(memory_space=pltpu.VMEM),),
        scratch_shapes=[
            pltpu.VMEM((rows, padded(rows)), F32),
            pltpu.VMEM((padded(rows), 2 * NB), BF16),
            pltpu.VMEM((NB, 2 * NB), F32),
            pltpu.VMEM((contrib, contrib), F32),
            pltpu.SemaphoreType.DMA((6,)),
        ],
        compiler_params=pltpu.CompilerParams(vmem_limit_bytes=48 * 2**20),
    )(own_p, got_p, own_l, got_l, own_t, got_t)


def parent_kernel(
    count, picked, first, maps, own, got, first_schur, others, diag_in, diag_got, below_in,
    below_got, out, diag, below, front, panel, work, block, sems, late_sems,
):
    member = lax.axis_index("front")
    half, pivots = got.shape
    contrib = first_schur.shape[0]
    mine = pl.multiple_of(member * half, 8)
    theirs = pl.multiple_of((1 - member) * half, 8)
    pivot_cols = pl.ds(0, pivots)
    copies = [
        pltpu.make_async_copy(own.at[0], front.at[pl.ds(mine, half), pivot_cols], sems.at[0]),
        pltpu.make_async_copy(got, front.at[pl.ds(theirs, half), pivot_cols], sems.at[1]),
    ]
    for copy in copies:
        copy.start()
    for copy in copies:
        copy.wait()
    late = [
        pltpu.make_async_copy(diag_got, diag.at[1 - member], late_sems.at[0]),
        pltpu.make_async_copy(below_got, below.at[1 - member], late_sems.at[1]),
    ]
    for copy in late:
        copy.start()
    slot = lax.broadcasted_iota(jnp.int32, (pivots, contrib), 0)
    strip = 3 * NB

    def place(child, values):
        places = jnp.where(slot == maps[pl.ds(child, 1), :], 1.0, 0.0).astype(BF16)
        high, low = split(values)
        spread_high = rows_dot(high, places).astype(BF16)
        spread_low = rows_dot(low, places).astype(BF16)
        for row in range(0, pivots, strip):
            for col in range(0, row + strip, strip):
                chosen = places[row : row + strip]
                front[row : row + strip, col : col + strip] = (
                    front[row : row + strip, col : col + strip]
                    + jnp.dot(
                        chosen, spread_high[:, col : col + strip], preferred_element_type=F32
                    )
                    + jnp.dot(chosen, spread_low[:, col : col + strip], preferred_element_type=F32)
                )

    block[...] = first_schur[...]

    def add(position, carry):
        @pl.when(position > 0)
        def _():
            source = picked[jnp.maximum(position - 1, 0)]
            copy = pltpu.make_async_copy(others.at[source], block, sems.at[0])
            copy.start()
            copy.wait()

        child = jnp.where(
            position > 0, picked[jnp.maximum(position - 1, 0)] * 2 + 1, first[0] * 2
        )
        place(child, unpack(block[...]))
        return carry

    lax.fori_loop(0, count[0] + 1, add, 0)
    factor_front(front, panel, work, pivots, pivots)
    copy = pltpu.make_async_copy(front.at[pl.ds(mine, half), pivot_cols], out.at[0], sems.at[0])
    copy.start()
    copy.wait()
    for copy in late:
        copy.wait()


def eliminate_parent(
    count, picked, first, maps, own, got, first_schur, others, diag, diag_got, below, below_got
):
    half, pivots = got.shape
    anywhere = pl.BlockSpec(memory_space=pl.ANY)
    scalars = pl.BlockSpec(memory_space=pltpu.SMEM)
    vmem = pl.BlockSpec(memory_space=pltpu.VMEM)
    return pl.pallas_call(
        parent_kernel,
        out_shape=(
            jax.ShapeDtypeStruct(own.shape, F32),
            jax.ShapeDtypeStruct(diag.shape, F32),
            jax.ShapeDtypeStruct(below.shape, F32),
        ),
        in_specs=[scalars] * 3 + [vmem, anywhere, anywhere, vmem] + [anywhere] * 5,
        out_specs=(anywhere,) * 3,
        input_output_aliases={8: 1, 10: 2},
        scratch_shapes=[
            pltpu.VMEM((pivots, padded(pivots)), F32),
            pltpu.VMEM((padded(pivots), 2 * NB), BF16),
            pltpu.VMEM((NB, 2 * NB), F32),
            pltpu.VMEM(first_schur.shape, F32),
            pltpu.SemaphoreType.DMA((2,)),
            pltpu.SemaphoreType.DMA((2,)),
        ],
        compiler_params=pltpu.CompilerParams(vmem_limit_bytes=48 * 2**20),
    )(
        count, picked, first, maps, own, got, first_schur, others, diag, diag_got, below, below_got
    )


def on_device(child_pivot, child_lower, child_tail, child_map, child_parent, owner, parent_front):
    member = lax.axis_index("front")
    group = lax.axis_index("leaf")
    groups = lax.axis_size("leaf")
    swap = [(0, 1), (1, 0)]

    def theirs(array):
        return lax.dynamic_index_in_dim(array, 1 - member, 0, keepdims=False)

    got_pivot = lax.ppermute(theirs(child_pivot), "front", swap)
    got_lower = lax.ppermute(theirs(child_lower), "front", swap)
    got_tail = lax.ppermute(theirs(child_tail), "front", swap)
    got_parent = lax.ppermute(parent_front[0], "front", swap)
    diag, diag_send, below, below_send, schur = eliminate_child(
        child_pivot, got_pivot, child_lower, got_lower, child_tail, got_tail
    )
    first_schur, others = exchange(schur, groups)
    diag_got = lax.ppermute(diag_send, "front", swap)
    below_got = lax.ppermute(below_send, "front", swap)

    mine = owner[child_parent[1::2, 0]] == group
    positions = jnp.arange(groups, dtype=jnp.int32)
    earlier = positions[None, :] < positions[:, None]
    rank = jnp.sum((earlier & mine[None, :]).astype(jnp.int32), axis=1)
    picked = jnp.sum(
        jnp.where((rank[None, :] == positions[:, None]) & mine[None, :], positions[None, :], 0),
        axis=1,
    ).astype(jnp.int32)
    count = jnp.sum(mine.astype(jnp.int32)).reshape(1)
    first = ((group + groups - groups // 2) % groups).astype(jnp.int32).reshape(1)
    parent, diag, below = eliminate_parent(
        count, picked, first, child_map, parent_front, got_parent, first_schur, others,
        diag, diag_got, below, below_got,
    )
    return (diag, below, parent)


def solution(mesh):
    in_specs = (
        P("leaf", "front", None),
        P("leaf", "front", None),
        P("leaf", "front", None),
        P(),
        P(),
        P(),
        P("leaf", "front", None),
    )
    out_specs = (P("leaf", "front", None), P("leaf", "front", None), P("leaf", "front", None))
    return jax.shard_map(
        on_device, mesh=mesh, in_specs=in_specs, out_specs=out_specs, check_vma=False
    )
```
